32 devices in a mesh: dp: 4 (over z), expert: 8 (over y, x, core).
Axes of the slice: x: 2, y: 2, z: 4, core: 2. Of those that a mesh axis runs over, the one named last changes fastest.
Arguments:
- tokens: bfloat16 [2048, 2048], P(('dp', 'expert')), may hold values from -6 to 6
- routes: int32 [2048, 4], P(('dp', 'expert')), may hold values from 0 to 59, all different within a row; in each aligned block of 64 rows (0 to 63, 64 to 127, ...) at most 5 rows name the same one
- route_weight: float32 [2048, 4], P(('dp', 'expert')), may hold values from 0.05 to 0.6
- expert_in: bfloat16 [64, 2, 1408, 2048], P('expert', None, 'dp'), may hold values from -0.125 to 0.125
- expert_out: bfloat16 [64, 1408, 2048], P('expert', None, 'dp'), may hold values from -0.15625 to 0.15625
Outputs:
- mixed: bfloat16 [2048, 2048], P(('dp', 'expert'))
The draws below stay inside these ranges and needn't reach their ends.
Inputs may be any that keep to these rules, and one draw needn't show every extreme that they name: `routes`: within the 64 rows of one device no expert is named by more than 5 rows, and some expert reaches 5 in some device's rows; only experts below 60 are named.
All inputs are finite; a program needn't handle non-finite values.
Results may differ from the reference program's by a relative error of at most 0.0057.
Values may be sent and summed in bfloat16 or wider, within the bound.
A program may use at most 128 MiB of HBM per device.

```python
import math
import jax
import jax.numpy as jnp
import numpy as np
from jax import lax

D = 2048
FF_E = 1408
E = 60
TOPK = 4
EP = 64
TOK_DEV = 64
MOST = 5
TOKENS = 2048
N_DP = 4
N_EXPERT = 8


def levels(rng, shape, shards, least, largest):
    level, own = 1.0, jax.random.fold_in(rng, 6)
    for dim, shards_of in shards:
        steps = jnp.exp(jax.random.uniform(jax.random.fold_in(own, dim), (shards_of,), jnp.float32, least / len(shards), largest / len(shards)))
        level = level * jnp.repeat(steps, shape[dim] // shards_of).reshape([-1 if axis == dim else 1 for axis in range(len(shape))])
    return level


def routed_block(stream_key, own, number, rows, number_of, top, limit, slope):
    order = jax.random.permutation(stream_key, number_of)
    heavy_load, usual = load_shares(number_of, rows * top, limit, slope, True), load_shares(number_of, rows * top, limit, slope, False)
    places = jnp.arange(number_of)

    def named(sizes, offset_by):
        used = int((sizes > 0).sum())
        fixed = max(1, used // 4)
        passed = fixed + (places - fixed + offset_by * (used - fixed)) % max(1, number_of - fixed)
        return jnp.zeros((number_of,), jnp.int32).at[order[jnp.where(places < fixed, places, passed)]].set(jnp.asarray(sizes, jnp.int32))

    sizes = jnp.where(number % 4 == 0, named(heavy_load, number // 4), named(usual, number - number // 4 - 1))
    mixed = jax.random.permutation(jax.random.fold_in(own, 3), number_of)
    source_of, sink = mixed[0:number_of // 2 * 2:2], mixed[1:number_of // 2 * 2:2]
    margin = jnp.minimum(sizes[source_of] - 1, limit - sizes[sink]) // 2
    margin = jnp.where((source_of == order[0]) | (sink == order[0]) | (sizes[sink] == 0), 0, jnp.maximum(margin, 0))
    passed = jax.random.randint(jax.random.fold_in(own, 4), (number_of // 2,), 0, 1 << 20) % (margin + 1)
    sizes = sizes.at[source_of].add(-passed).at[sink].add(passed)
    items = jnp.searchsorted(jnp.cumsum(sizes), jnp.arange(rows * top), side="right").astype(jnp.int32)
    table = items.reshape(top, rows).T
    table = table[jax.random.permutation(jax.random.fold_in(own, 1), rows)]
    offset_by = jax.random.randint(jax.random.fold_in(own, 2), (rows, 1), 0, top)
    return jnp.take_along_axis(table, (jnp.arange(top)[None, :] + offset_by) % top, axis=1)


def load_shares(number_of, total, limit, lean, full):
    portions = [(1 << 20) // math.isqrt(grade ** lean) + 1 for grade in range(1, number_of + 1)]
    largest = limit if full else min(limit, max(-(-total // number_of), total * portions[0] // sum(portions)))
    least = 1 if total - largest >= number_of - 1 else 0
    holding, surplus = [largest] + [least] * (number_of - 1), total - largest - least * (number_of - 1)
    while surplus > 0:
        movable = [i for i in range(1, number_of) if holding[i] < largest] or [i for i in range(1, number_of) if holding[i] < limit]
        pool, budget = sum([portions[i] for i in movable]), surplus
        for i in movable:
            more = min(limit - holding[i], max(1, budget * portions[i] // pool), surplus)
            holding[i] = holding[i] + more
            surplus = surplus - more
    return np.array(holding)


def scatter_about(key, extent, spread, limit, shards=(), kind=jnp.bfloat16):
    values = jax.random.normal(key, extent, jnp.float32) * spread
    if len(shards) > 0:
        values = levels(key, extent, shards, -0.22, 0.18) * values
    return jnp.clip(values, min=-limit, max=limit).astype(kind)


def setup_inputs(seed: int = 0) -> dict:
    keys = jax.random.split(jax.random.key(seed), 6)
    tokens = scatter_about(keys[0], (TOKENS, D), 1.0, 6.0, ((0, 32),))
    routes_keys = jax.random.split(jax.random.fold_in(keys[1], 1), TOKENS // TOK_DEV)
    routes_turns = jax.random.permutation(jax.random.fold_in(keys[1], 3), TOKENS // TOK_DEV)
    routes = jax.vmap(lambda own, number: routed_block(jax.random.fold_in(keys[1], 2), own, number, TOK_DEV, E, TOPK, MOST, 2))(routes_keys, routes_turns).reshape((TOKENS, TOPK))
    route_weight = jnp.clip(jnp.exp(math.log(0.6) - 2.4849067 * jax.random.uniform(keys[2], (TOKENS, TOPK), jnp.float32) ** levels(keys[2], (TOKENS, TOPK), ((0, 32),), -0.2, 0.2)), 0.05, 0.6)
    expert_in = scatter_about(keys[3], (EP, 2, FF_E, D), D ** -0.5, 0.125, ((0, 8), (2, 4)))
    expert_out = scatter_about(keys[4], (EP, FF_E, D), FF_E ** -0.5, 0.15625, ((0, 8), (2, 4)))
    return dict(tokens=tokens, routes=routes, route_weight=route_weight, expert_in=expert_in, expert_out=expert_out)


def reference(tokens, routes, route_weight, expert_in, expert_out):
    flat = routes.reshape(-1)
    weights_flat = route_weight.reshape(-1)
    capacity = MOST * N_DP * N_EXPERT

    def one_expert(carry, expert):
        match = flat == expert
        count = jnp.sum(match.astype(jnp.int32))
        where = jnp.nonzero(match, size=capacity, fill_value=0)[0]
        valid = (jnp.arange(capacity) < count).astype(jnp.float32)
        owner = where // TOPK
        rows = tokens[owner]
        both = expert_in[expert]
        gate = jnp.dot(rows, both[0].T, preferred_element_type=jnp.float32)
        up = jnp.dot(rows, both[1].T, preferred_element_type=jnp.float32)
        hidden = (jax.nn.silu(gate) * up).astype(jnp.bfloat16)
        output = jnp.dot(hidden, expert_out[expert], preferred_element_type=jnp.float32).astype(jnp.bfloat16)
        scale = weights_flat[where] * valid
        carry = carry.at[owner].add(scale[:, None] * output.astype(jnp.float32))
        return carry, None

    start = jnp.zeros((tokens.shape[0], tokens.shape[1]), jnp.float32)
    total, unused = lax.scan(one_expert, start, jnp.arange(E, dtype=jnp.int32))
    return total.astype(jnp.bfloat16)
```

```python
import functools

import jax
import jax.numpy as jnp
from jax import lax
from jax.experimental import pallas as pl
from jax.experimental.pallas import tpu as pltpu
from jax.sharding import PartitionSpec as P

MOST = 5
META = 128
MESH = pl.DeviceIdType.MESH


def slot_parts(route_rows):
    flat = route_rows.reshape(-1)
    order = jnp.arange(flat.shape[0], dtype=jnp.int32)
    earlier = (flat[:, None] == flat[None, :]) & (order[None, :] < order[:, None])
    return (flat, jnp.sum(earlier.astype(jnp.int32), axis=1))


def pack_rows(source_rows, target, owner, slot_count):
    filled = jnp.zeros((slot_count,), jnp.int32).at[target].set(owner + 1)
    picked = source_rows[jnp.maximum(filled - 1, 0)]
    return jnp.where((filled > 0)[:, None], picked, jnp.zeros_like(picked))


def local(tokens, routes, route_weight, expert_in, expert_out):
    dp_count = lax.axis_size("dp")
    col_count = lax.axis_size("expert")
    local_experts = expert_in.shape[0]
    tok_count = tokens.shape[0]
    route_count = routes.shape[1]
    features = tokens.shape[1]
    slice_width = expert_out.shape[2]
    pair_count = tok_count * route_count
    chosen, rank = slot_parts(routes)
    own_slot = chosen % local_experts * (col_count * MOST) + chosen // local_experts * MOST + rank
    owner = jnp.arange(pair_count, dtype=jnp.int32) // route_count
    packed = pack_rows(tokens, own_slot, owner, local_experts * col_count * MOST)
    packed = packed.reshape(local_experts, col_count, MOST * features)
    arrived = lax.all_to_all(packed, "expert", split_axis=1, concat_axis=1, tiled=True)
    arrived = arrived.reshape(local_experts, col_count * MOST, features)
    both = jnp.einsum(
        "erd,egfd->gefr",
        lax.all_gather(arrived, "dp", axis=1, tiled=True),
        expert_in,
        preferred_element_type=jnp.float32,
    )
    hidden = (jax.nn.silu(both[0]) * both[1]).astype(jnp.bfloat16)
    piece = lax.all_gather(hidden, "dp", axis=1, tiled=True)
    width = piece.shape[1]
    blocks = piece.reshape(local_experts, width, dp_count, col_count, MOST)
    outputs = jnp.einsum(
        "efabm,efd->ebmad", blocks, expert_out, preferred_element_type=jnp.float32
    ).astype(jnp.bfloat16)
    outputs = outputs.reshape(local_experts, col_count, MOST, dp_count * slice_width)
    returned = lax.all_to_all(
        lax.all_to_all(outputs, "dp", split_axis=3, concat_axis=3, tiled=True),
        "expert",
        split_axis=1,
        concat_axis=1,
        tiled=True,
    )
    returned = returned.reshape(local_experts * col_count * MOST, features)
    picked = returned[own_slot].reshape(tok_count, route_count, features)
    mixed = jnp.sum(route_weight[:, :, None] * picked.astype(jnp.float32), axis=1)
    return mixed.astype(jnp.bfloat16)


def gather_kernel(n, cols, own_ref, out_ref, own_sem, send_sem, recv_sem):
    z, c = lax.axis_index("dp"), lax.axis_index("expert")
    sib_of = lambda col: col + 1 - 2 * (col % 2)
    xn = c + 2 - 4 * ((c // 2) % 2)
    yn = c + 4 - 8 * (c // 4)
    diag = xn + 4 - 8 * (xn // 4)
    sib = sib_of(c)
    half = own_ref.shape[0] // 2

    barrier = pltpu.get_barrier_semaphore()
    for col in (xn, yn, sib):
        pl.semaphore_signal(barrier, inc=1, device_id=(z, col), device_id_type=MESH)

    @pl.when(z > 0)
    def _():
        pl.semaphore_signal(barrier, inc=1, device_id=(z - 1, c), device_id_type=MESH)

    @pl.when(z < n - 1)
    def _():
        pl.semaphore_signal(barrier, inc=1, device_id=(z + 1, c), device_id_type=MESH)

    own = pltpu.make_async_copy(own_ref, out_ref.at[z * cols + c], own_sem)
    own.start()
    own.wait()
    pl.semaphore_wait(barrier, 3 + (z > 0).astype(jnp.int32) + (z < n - 1).astype(jnp.int32))

    def copy(block, kind, target, part=None):
        if part is None:
            ref, sem = out_ref.at[block], recv_sem.at[block, 0]
        else:
            ref, sem = out_ref.at[block, pl.ds(part * half, half)], recv_sem.at[block, part]
        return pltpu.make_async_remote_copy(
            src_ref=ref, dst_ref=ref, send_sem=send_sem.at[block, kind], recv_sem=sem,
            device_id=target, device_id_type=MESH,
        )

    def along_z(off, go):
        zz = z + off
        block = zz * cols + c
        if off <= 0:
            @pl.when(z < n - 1)
            def _():
                go(copy(block, 0, (z + 1, c)))
        if off >= 0:
            @pl.when(z > 0)
            def _():
                go(copy(block, 1, (z - 1, c)))
        go(copy(block, 2, (z, xn)))
        go(copy(block, 3, (z, yn)))
        go(copy(block, 4, (z, sib)))

    def in_plane(off, go, wait):
        bx, by = (z + off) * cols + xn, (z + off) * cols + yn
        if wait:
            copy(bx, 0, (z, xn)).wait_recv()
        go(copy(bx, 0, (z, yn), 0))
        go(copy(bx, 4, (z, sib)))
        if wait:
            copy(by, 0, (z, yn)).wait_recv()
        go(copy(by, 0, (z, xn), 1))
        go(copy(by, 4, (z, sib)))

    def across(off, go, wait):
        bd = (z + off) * cols + diag
        if wait:
            copy(bd, 0, (z, yn), 0).wait_recv()
            copy(bd, 1, (z, xn), 1).wait_recv()
        go(copy(bd, 4, (z, sib)))

    offs = [0]
    for d in range(1, n):
        offs += [-d, d]
    start = lambda cp: cp.start()

    def on_slice(off, f):
        if off == 0:
            f()
        elif off < 0:
            pl.when(z + off >= 0)(f)
        else:
            pl.when(z + off < n)(f)

    for i in range(len(offs) + 2):
        if i < len(offs):
            def first(off=offs[i]):
                if off != 0:
                    copy((z + off) * cols + c, 0, (z, sib)).wait_recv()
                along_z(off, start)
            on_slice(offs[i], first)
        if 0 <= i - 1 < len(offs):
            on_slice(offs[i - 1], functools.partial(in_plane, offs[i - 1], start, True))
        if i >= 2:
            on_slice(offs[i - 2], functools.partial(across, offs[i - 2], start, True))

    sent = lambda cp: cp.wait_send()
    for off in offs:
        def last(off=off):
            for col in (c, xn, yn, diag):
                copy((z + off) * cols + sib_of(col), 0, (z, sib)).wait_recv()
            along_z(off, sent)
            in_plane(off, sent, False)
            across(off, sent, False)
        on_slice(off, last)


def expert_kernel(
    n, cols, x_ref, win_ref, wout_ref, perm_ref, weight_ref, out_ref,
    win, wout, hid, outs, msg, got, win_sem, wout_sem, hid_send, hid_recv, msg_send, msg_recv,
):
    z, c = lax.axis_index("dp"), lax.axis_index("expert")
    me = z * cols + c
    total = n * cols
    experts, rows = win.shape[0], hid.shape[2]
    features = win.shape[3]
    width = outs.shape[1]

    @pl.loop(0, experts)
    def _(e):
        pltpu.make_async_copy(win_ref.at[e], win.at[e], win_sem.at[e]).start()

    @pl.loop(0, experts)
    def _(e):
        pltpu.make_async_copy(wout_ref.at[e], wout.at[e], wout_sem.at[e]).start()

    barrier = pltpu.get_barrier_semaphore()

    @pl.loop(1, total)
    def _(d):
        other = (me + d) % total
        pl.semaphore_signal(barrier, inc=1, device_id=(other // cols, other % cols), device_id_type=MESH)

    pl.semaphore_wait(barrier, total - 1)

    def pass_on(zz, e, way, target):
        return pltpu.make_async_remote_copy(
            src_ref=hid.at[zz, e], dst_ref=hid.at[zz, e], send_sem=hid_send.at[zz, e, way],
            recv_sem=hid_recv.at[zz, e], device_id=(target, c), device_id_type=MESH,
        )

    def upward(zz, e):
        @pl.when(z < n - 1)
        def _():
            pass_on(zz, e, 0, z + 1).start()

    def downward(zz, e):
        @pl.when(z > 0)
        def _():
            pass_on(zz, e, 1, z - 1).start()

    contract_last = (((1,), (1,)), ((), ()))

    @pl.loop(0, experts + n - 1)
    def _(i):
        @pl.when(i < experts)
        def _():
            pltpu.make_async_copy(win_ref.at[i], win.at[i], win_sem.at[i]).wait()
            x = x_ref[:, i, :, :features].reshape(rows, features)
            gate = lax.dot_general(x, win[i, 0], contract_last, preferred_element_type=jnp.float32)
            up = lax.dot_general(x, win[i, 1], contract_last, preferred_element_type=jnp.float32)
            hid[z, i] = (gate / (1.0 + jnp.exp(-gate)) * up).astype(jnp.bfloat16)
            upward(z, i)
            downward(z, i)

        for d in range(1, n):
            e = i - d

            @pl.when((e >= 0) & (e < experts) & (z - d >= 0))
            def _():
                pass_on(z - d, e, 0, (z + 1) % n).wait_recv()
                upward(z - d, e)

            @pl.when((e >= 0) & (e < experts) & (z + d < n))
            def _():
                pass_on(z + d, e, 1, (z + 1) % n).wait_recv()
                downward(z + d, e)

        @pl.when(i >= n - 1)
        def _():
            e = i - (n - 1)
            pltpu.make_async_copy(wout_ref.at[e], wout.at[e], wout_sem.at[e]).wait()
            acc = jnp.zeros((rows, width), jnp.float32)
            for zz in range(n):
                acc += jnp.dot(hid[zz, e], wout[e, zz], preferred_element_type=jnp.float32)
            outs[pl.ds(pl.multiple_of(e * rows, rows), rows), :] = acc.astype(jnp.bfloat16)

    def message(dest):
        return pltpu.make_async_remote_copy(
            src_ref=msg.at[dest], dst_ref=got.at[me], send_sem=msg_send.at[dest],
            recv_sem=msg_recv.at[me], device_id=(dest // cols, dest % cols), device_id_type=MESH,
        )

    slots = msg.shape[1]

    @pl.loop(0, n)
    def _(j):
        zz = (z + 1 + j) % n
        part = perm_ref[pl.ds(pl.multiple_of(zz * (cols * slots), cols * slots), cols * slots), :]
        lanes = lax.broadcasted_iota(jnp.int32, (cols * slots, outs.shape[0]), 1)
        pick = jnp.where(lanes == part, 1.0, 0.0).astype(jnp.bfloat16)
        moved = jnp.dot(pick, outs[...], preferred_element_type=jnp.float32)
        msg[pl.ds(zz * cols, cols)] = moved.reshape(cols, slots, width).astype(jnp.bfloat16)

        @pl.loop(0, cols)
        def _(k):
            dest = zz * cols + (c + k) % cols

            @pl.when(dest != me)
            def _():
                message(dest).start()

    got[me] = msg[me]

    @pl.loop(1, total)
    def _(d):
        source = (me + d) % total
        pltpu.make_async_remote_copy(
            src_ref=msg.at[source], dst_ref=got.at[source], send_sem=msg_send.at[source],
            recv_sem=msg_recv.at[source], device_id=(source // cols, source % cols), device_id_type=MESH,
        ).wait_recv()

    tok = out_ref.shape[0]
    for zz in range(n):
        acc = jnp.zeros((2 * tok, width), jnp.float32)
        for col in range(cols):
            acc += jnp.dot(weight_ref[col], got[zz * cols + col], preferred_element_type=jnp.float32)
        out_ref[:, zz * width:(zz + 1) * width] = (acc[:tok] + acc[tok:]).astype(jnp.bfloat16)

    @pl.loop(1, total)
    def _(d):
        message((me + d) % total).wait_send()

    @pl.loop(0, experts)
    def _(e):
        for zz in range(n):
            @pl.when((z < n - 1) & (zz <= z))
            def _():
                pass_on(zz, e, 0, z + 1).wait_send()

            @pl.when((z > 0) & (zz >= z))
            def _():
                pass_on(zz, e, 1, z - 1).wait_send()


def fused(n, cols, tokens, routes, route_weight, expert_in, expert_out):
    tok, features = tokens.shape
    top = routes.shape[1]
    experts, _, hidden, _ = expert_in.shape
    width = expert_out.shape[2]
    total = n * cols
    col = lax.axis_index("expert")
    slots = experts * MOST
    rows = total * MOST

    chosen, rank = slot_parts(routes)
    rank = rank.reshape(tok, top)
    meta = jnp.concatenate([routes, rank, jnp.zeros((tok, META - 2 * top), jnp.int32)], axis=1)
    block = jnp.concatenate([tokens, meta.astype(jnp.bfloat16)], axis=1)
    gathered = pl.pallas_call(
        functools.partial(gather_kernel, n, cols),
        out_shape=jax.ShapeDtypeStruct((total, tok, features + META), jnp.bfloat16),
        in_specs=[pl.BlockSpec(memory_space=pl.ANY)],
        out_specs=pl.BlockSpec(memory_space=pl.ANY),
        scratch_shapes=[
            pltpu.SemaphoreType.DMA,
            pltpu.SemaphoreType.DMA((total, 5)),
            pltpu.SemaphoreType.DMA((total, 2)),
        ],
        compiler_params=pltpu.CompilerParams(collective_id=0, has_side_effects=True),
    )(block)

    groups = 2
    per_group = rows // groups
    seen = gathered[:, :, features:features + 2 * top].astype(jnp.int32)
    expert = col * experts + jnp.arange(experts, dtype=jnp.int32)
    base = (jnp.arange(total, dtype=jnp.int32) % (total // groups)) * MOST
    slot = seen[:, :, top:] + base[:, None, None] + 1
    match = seen[None, :, :, :top] == expert[:, None, None, None]
    place = jnp.sum(jnp.where(match, slot[None], 0), axis=3) - 1
    place = place.reshape(experts, groups, total // groups * tok).transpose(1, 0, 2)
    pick = place[:, :, None, :] == jnp.arange(per_group, dtype=jnp.int32)[None, None, :, None]
    x = jnp.einsum(
        "gst,gtd->gsd",
        pick.astype(jnp.bfloat16).reshape(groups, experts * per_group, -1),
        gathered.reshape(groups, total // groups * tok, features + META),
        preferred_element_type=jnp.bfloat16,
    ).reshape(groups, experts, per_group, features + META)

    order = jnp.arange(total * slots, dtype=jnp.int32)
    perm = (order % slots // MOST * rows + order // slots * MOST + order % MOST)[:, None]
    spot = (chosen * MOST).reshape(tok, top) + rank
    exact = jnp.sum(
        jnp.where(
            spot[:, :, None] == jnp.arange(cols * slots, dtype=jnp.int32), route_weight[:, :, None], 0.0
        ),
        axis=1,
    )
    high = lax.reduce_precision(exact, 8, 7)
    weight = jnp.concatenate([high, exact - high], axis=0).astype(jnp.bfloat16)
    weight = weight.reshape(2 * tok, cols, slots).transpose(1, 0, 2)

    vmem = pl.BlockSpec(memory_space=pltpu.VMEM)
    anywhere = pl.BlockSpec(memory_space=pl.ANY)
    return pl.pallas_call(
        functools.partial(expert_kernel, n, cols),
        out_shape=jax.ShapeDtypeStruct((tok, features), jnp.bfloat16),
        in_specs=[vmem, anywhere, anywhere, vmem, vmem],
        out_specs=vmem,
        scratch_shapes=[
            pltpu.VMEM((experts, 2, hidden, features), jnp.bfloat16),
            pltpu.VMEM((experts, n, hidden, width), jnp.bfloat16),
            pltpu.VMEM((n, experts, rows, hidden), jnp.bfloat16),
            pltpu.VMEM((experts * rows, width), jnp.bfloat16),
            pltpu.VMEM((total, slots, width), jnp.bfloat16),
            pltpu.VMEM((total, slots, width), jnp.bfloat16),
            pltpu.SemaphoreType.DMA((experts,)),
            pltpu.SemaphoreType.DMA((experts,)),
            pltpu.SemaphoreType.DMA((n, experts, 2)),
            pltpu.SemaphoreType.DMA((n, experts)),
            pltpu.SemaphoreType.DMA((total,)),
            pltpu.SemaphoreType.DMA((total,)),
        ],
        compiler_params=pltpu.CompilerParams(
            collective_id=1, has_side_effects=True, vmem_limit_bytes=60 * 1024 * 1024
        ),
    )(x, expert_in, expert_out.reshape(experts, n, hidden, width), perm, weight)


def solution(mesh):
    n, cols = mesh.shape["dp"], mesh.shape["expert"]

    def body(*args):
        if n * cols > 32 or cols != 8:
            return local(*args)
        return fused(n, cols, *args)

    return jax.shard_map(
        body,
        mesh=mesh,
        in_specs=(
            P(("dp", "expert"), None),
            P(("dp", "expert"), None),
            P(("dp", "expert"), None),
            P("expert", None, "dp", None),
            P("expert", None, "dp"),
        ),
        out_specs=P(("dp", "expert"), None),
        check_vma=False,
    )
```

```python
import functools

import jax
import jax.numpy as jnp
from jax import lax
from jax.experimental import pallas as pl
from jax.experimental.pallas import tpu as pltpu
from jax.sharding import PartitionSpec as P

MOST = 5
MESH = pl.DeviceIdType.MESH


def slot_parts(route_rows):
    flat = route_rows.reshape(-1)
    order = jnp.arange(flat.shape[0], dtype=jnp.int32)
    earlier = (flat[:, None] == flat[None, :]) & (order[None, :] < order[:, None])
    return (flat, jnp.sum(earlier.astype(jnp.int32), axis=1))


def pack_rows(source_rows, target, owner, slot_count):
    filled = jnp.zeros((slot_count,), jnp.int32).at[target].set(owner + 1)
    picked = source_rows[jnp.maximum(filled - 1, 0)]
    return jnp.where((filled > 0)[:, None], picked, jnp.zeros_like(picked))


def local(tokens, routes, route_weight, expert_in, expert_out):
    dp_count = lax.axis_size("dp")
    col_count = lax.axis_size("expert")
    local_experts = expert_in.shape[0]
    tok_count = tokens.shape[0]
    route_count = routes.shape[1]
    features = tokens.shape[1]
    slice_width = expert_out.shape[2]
    pair_count = tok_count * route_count
    chosen, rank = slot_parts(routes)
    own_slot = chosen % local_experts * (col_count * MOST) + chosen // local_experts * MOST + rank
    owner = jnp.arange(pair_count, dtype=jnp.int32) // route_count
    packed = pack_rows(tokens, own_slot, owner, local_experts * col_count * MOST)
    packed = packed.reshape(local_experts, col_count, MOST * features)
    arrived = lax.all_to_all(packed, "expert", split_axis=1, concat_axis=1, tiled=True)
    arrived = arrived.reshape(local_experts, col_count * MOST, features)
    both = jnp.einsum(
        "erd,egfd->gefr",
        lax.all_gather(arrived, "dp", axis=1, tiled=True),
        expert_in,
        preferred_element_type=jnp.float32,
    )
    hidden = (jax.nn.silu(both[0]) * both[1]).astype(jnp.bfloat16)
    piece = lax.all_gather(hidden, "dp", axis=1, tiled=True)
    width = piece.shape[1]
    blocks = piece.reshape(local_experts, width, dp_count, col_count, MOST)
    outputs = jnp.einsum(
        "efabm,efd->ebmad", blocks, expert_out, preferred_element_type=jnp.float32
    ).astype(jnp.bfloat16)
    outputs = outputs.reshape(local_experts, col_count, MOST, dp_count * slice_width)
    returned = lax.all_to_all(
        lax.all_to_all(outputs, "dp", split_axis=3, concat_axis=3, tiled=True),
        "expert",
        split_axis=1,
        concat_axis=1,
        tiled=True,
    )
    returned = returned.reshape(local_experts * col_count * MOST, features)
    picked = returned[own_slot].reshape(tok_count, route_count, features)
    mixed = jnp.sum(route_weight[:, :, None] * picked.astype(jnp.float32), axis=1)
    return mixed.astype(jnp.bfloat16)


def line_kernel(n, own_ref, out_ref, own_sem, send_sem, recv_sem):
    z, c = lax.axis_index("dp"), lax.axis_index("expert")
    barrier = pltpu.get_barrier_semaphore()

    @pl.when(z > 0)
    def _():
        pl.semaphore_signal(barrier, inc=1, device_id=(z - 1, c), device_id_type=MESH)

    @pl.when(z < n - 1)
    def _():
        pl.semaphore_signal(barrier, inc=1, device_id=(z + 1, c), device_id_type=MESH)

    own = pltpu.make_async_copy(own_ref, out_ref.at[z], own_sem)
    own.start()
    pl.semaphore_wait(barrier, (z > 0).astype(jnp.int32) + (z < n - 1).astype(jnp.int32))

    def copy(zz, way, target, first=False):
        return pltpu.make_async_remote_copy(
            src_ref=own_ref if first else out_ref.at[zz], dst_ref=out_ref.at[zz],
            send_sem=send_sem.at[zz, way], recv_sem=recv_sem.at[zz],
            device_id=(target, c), device_id_type=MESH,
        )

    @pl.when(z < n - 1)
    def _():
        copy(z, 0, z + 1, True).start()

    @pl.when(z > 0)
    def _():
        copy(z, 1, z - 1, True).start()

    for d in range(1, n):
        @pl.when(z - d >= 0)
        def _():
            copy(z - d, 0, (z + 1) % n).wait_recv()

            @pl.when(z < n - 1)
            def _():
                copy(z - d, 0, z + 1).start()

        @pl.when(z + d < n)
        def _():
            copy(z + d, 1, (z + 1) % n).wait_recv()

            @pl.when(z > 0)
            def _():
                copy(z + d, 1, z - 1).start()

    own.wait()
    for zz in range(n):
        @pl.when((z < n - 1) & (zz <= z))
        def _():
            copy(zz, 0, z + 1).wait_send()

        @pl.when((z > 0) & (zz >= z))
        def _():
            copy(zz, 1, z - 1).wait_send()


def expert_kernel(
    n, cols, groups, line_ref, place_ref, win_ref, wout_ref, perm_ref, weight_ref, out_ref,
    win, wout, tokens, pick, x, hid, outs, msg, got,
    win_sem, wout_sem, own_sem, tok_send, tok_recv, hid_send, hid_recv, msg_send, msg_recv,
):
    z, c = lax.axis_index("dp"), lax.axis_index("expert")
    me = z * cols + c
    total = n * cols
    experts, rows = win.shape[0], hid.shape[2]
    steps = groups * experts
    xn = c + 2 - 4 * ((c // 2) % 2)
    yn = c + 4 - 8 * (c // 4)
    diag = xn + 4 - 8 * (xn // 4)
    sib = c + 1 - 2 * (c % 2)
    half = tokens.shape[1] // 2
    features = win.shape[3]
    width = outs.shape[1]

    barrier = pltpu.get_barrier_semaphore()

    @pl.loop(1, total)
    def _(d):
        other = (me + d) % total
        pl.semaphore_signal(barrier, inc=1, device_id=(other // cols, other % cols), device_id_type=MESH)

    pl.semaphore_wait(barrier, total - 1)

    def own_block(zz):
        return pltpu.make_async_copy(line_ref.at[zz], tokens.at[zz * cols + c], own_sem.at[zz])

    def share(zz, col, kind, target, part=None):
        block = zz * cols + col
        dst, sem = tokens.at[block], tok_recv.at[block, 0]
        src = line_ref.at[zz] if kind < 3 else dst
        if part is not None:
            src = dst = tokens.at[block, pl.ds(part * half, half)]
            sem = tok_recv.at[block, part]
        return pltpu.make_async_remote_copy(
            src_ref=src, dst_ref=dst, send_sem=tok_send.at[block, kind], recv_sem=sem,
            device_id=(z, target), device_id_type=MESH,
        )

    def offer(zz):
        return [share(zz, c, 0, xn), share(zz, c, 1, yn), share(zz, c, 2, sib)]

    def relay(zz):
        return [
            share(zz, xn, 3, yn, 0), share(zz, xn, 4, sib),
            share(zz, yn, 3, xn, 1), share(zz, yn, 4, sib),
        ]

    def begin(zz):
        own_block(zz).start()
        for cp in offer(zz):
            cp.start()

    def forward(zz):
        share(zz, xn, 4, sib).wait_recv()
        for cp in relay(zz)[:2]:
            cp.start()
        share(zz, yn, 4, sib).wait_recv()
        for cp in relay(zz)[2:]:
            cp.start()

    def across(zz):
        share(zz, diag, 3, yn, 0).wait_recv()
        share(zz, diag, 3, xn, 1).wait_recv()
        share(zz, diag, 4, sib).start()

    def complete(zz):
        own_block(zz).wait()
        for col in (sib, xn + 1 - 2 * (xn % 2), yn + 1 - 2 * (yn % 2), diag + 1 - 2 * (diag % 2)):
            share(zz, col, 4, sib).wait_recv()

    per = n // groups
    for zz in range(per):
        begin(zz)
    @pl.loop(0, experts)
    def _(e):
        pltpu.make_async_copy(win_ref.at[e], win.at[e], win_sem.at[e]).start()

    @pl.loop(0, experts)
    def _(e):
        pltpu.make_async_copy(wout_ref.at[e], wout.at[e], wout_sem.at[e]).start()

    for zz in range(per, n):
        begin(zz)
    for zz in range(per):
        forward(zz)
    for zz in range(per):
        across(zz)
    for zz in range(per):
        complete(zz)

    def choose(g):
        size = tokens.shape[1] * per * cols
        for e in range(experts):
            at = lax.broadcasted_iota(jnp.int32, (rows, size), 0)
            named = place_ref[g, e:e + 1, :]
            pick[e * rows:(e + 1) * rows, :] = jnp.where(at == named, 1.0, 0.0).astype(jnp.bfloat16)

        @pl.loop(0, features // width)
        def _(j):
            at = pl.ds(pl.multiple_of(j * width, width), width)
            part = tokens[pl.ds(g * (per * cols), per * cols), :, at].reshape(size, width)
            x[:, at] = jnp.dot(pick[...], part, preferred_element_type=jnp.float32).astype(jnp.bfloat16)

    def pass_on(zz, e, way, target):
        return pltpu.make_async_remote_copy(
            src_ref=hid.at[zz, e], dst_ref=hid.at[zz, e], send_sem=hid_send.at[zz, e, way],
            recv_sem=hid_recv.at[zz, e], device_id=(target, c), device_id_type=MESH,
        )

    def upward(zz, e):
        @pl.when(z < n - 1)
        def _():
            pass_on(zz, e, 0, z + 1).start()

    def downward(zz, e):
        @pl.when(z > 0)
        def _():
            pass_on(zz, e, 1, z - 1).start()

    contract_last = (((1,), (1,)), ((), ()))

    choose(0)

    @pl.loop(0, steps + n - 1)
    def _(i):
        for g in range(1, groups):
            for k in range(per):
                @pl.when(i == (g - 1) * experts + 1 + 2 * k)
                def _():
                    forward(g * per + k)

                @pl.when(i == (g - 1) * experts + 3 + 2 * k)
                def _():
                    across(g * per + k)

            @pl.when(i == g * experts)
            def _():
                for k in range(per):
                    complete(g * per + k)
                choose(g)

        @pl.when(i < experts)
        def _():
            pltpu.make_async_copy(win_ref.at[i], win.at[i], win_sem.at[i]).wait()

        @pl.when(i < steps)
        def _():
            e = i % experts
            xe = x[pl.ds(pl.multiple_of(e * rows, rows), rows), :]
            gate = lax.dot_general(xe, win[e, 0], contract_last, preferred_element_type=jnp.float32)
            up = lax.dot_general(xe, win[e, 1], contract_last, preferred_element_type=jnp.float32)
            hid[z, i] = (gate / (1.0 + jnp.exp(-gate)) * up).astype(jnp.bfloat16)
            upward(z, i)
            downward(z, i)

        for d in range(1, n):
            e = i - d

            @pl.when((e >= 0) & (e < steps) & (z - d >= 0))
            def _():
                pass_on(z - d, e, 0, (z + 1) % n).wait_recv()
                upward(z - d, e)

            @pl.when((e >= 0) & (e < steps) & (z + d < n))
            def _():
                pass_on(z + d, e, 1, (z + 1) % n).wait_recv()
                downward(z + d, e)

        @pl.when(i >= n - 1)
        def _():
            step = i - (n - 1)
            e = step % experts

            @pl.when(step < experts)
            def _():
                pltpu.make_async_copy(wout_ref.at[e], wout.at[e], wout_sem.at[e]).wait()

            acc = jnp.zeros((rows, width), jnp.float32)
            for zz in range(n):
                acc += jnp.dot(hid[zz, step], wout[e, zz], preferred_element_type=jnp.float32)
            row = pl.multiple_of(step * rows, rows)
            outs[pl.ds(row, rows), :] = acc.astype(jnp.bfloat16)

    def message(dest):
        return pltpu.make_async_remote_copy(
            src_ref=msg.at[dest], dst_ref=got.at[me], send_sem=msg_send.at[dest],
            recv_sem=msg_recv.at[me], device_id=(dest // cols, dest % cols), device_id_type=MESH,
        )

    slots = msg.shape[1]

    @pl.loop(0, n)
    def _(j):
        zz = (z + 1 + j) % n
        part = perm_ref[pl.ds(pl.multiple_of(zz * (cols * slots), cols * slots), cols * slots), :]
        lanes = lax.broadcasted_iota(jnp.int32, (cols * slots, outs.shape[0]), 1)
        pick = jnp.where(lanes == part, 1.0, 0.0).astype(jnp.bfloat16)
        moved = jnp.dot(pick, outs[...], preferred_element_type=jnp.float32)
        msg[pl.ds(zz * cols, cols)] = moved.reshape(cols, slots, width).astype(jnp.bfloat16)

        @pl.loop(0, cols)
        def _(k):
            dest = zz * cols + (c + k) % cols

            @pl.when(dest != me)
            def _():
                message(dest).start()

    got[me] = msg[me]

    @pl.loop(1, total)
    def _(d):
        source = (me + d) % total
        pltpu.make_async_remote_copy(
            src_ref=msg.at[source], dst_ref=got.at[source], send_sem=msg_send.at[source],
            recv_sem=msg_recv.at[source], device_id=(source // cols, source % cols), device_id_type=MESH,
        ).wait_recv()

    tok = out_ref.shape[0]
    for zz in range(n):
        acc = jnp.zeros((2 * tok, width), jnp.float32)
        for col in range(cols):
            acc += jnp.dot(weight_ref[col], got[zz * cols + col], preferred_element_type=jnp.float32)
        out_ref[:, zz * width:(zz + 1) * width] = (acc[:tok] + acc[tok:]).astype(jnp.bfloat16)

    @pl.loop(1, total)
    def _(d):
        message((me + d) % total).wait_send()

    @pl.loop(0, n)
    def _(zz):
        for cp in offer(zz) + relay(zz) + [share(zz, diag, 4, sib)]:
            cp.wait_send()

    @pl.loop(0, steps)
    def _(e):
        for zz in range(n):
            @pl.when((z < n - 1) & (zz <= z))
            def _():
                pass_on(zz, e, 0, z + 1).wait_send()

            @pl.when((z > 0) & (zz >= z))
            def _():
                pass_on(zz, e, 1, z - 1).wait_send()


def fused(n, cols, tokens, routes, route_weight, expert_in, expert_out):
    tok, features = tokens.shape
    top = routes.shape[1]
    experts, _, hidden, _ = expert_in.shape
    width = expert_out.shape[2]
    total = n * cols
    col = lax.axis_index("expert")
    slots = experts * MOST
    rows = total * MOST

    chosen, rank = slot_parts(routes)
    rank = rank.reshape(tok, top)
    meta = jnp.concatenate([routes, rank], axis=1).reshape(1, tok * 2 * top)
    seen = lax.all_gather(meta, ("dp", "expert"), axis=0, tiled=True).reshape(total, tok, 2 * top)
    line = pl.pallas_call(
        functools.partial(line_kernel, n),
        out_shape=jax.ShapeDtypeStruct((n, tok, features), jnp.bfloat16),
        in_specs=[pl.BlockSpec(memory_space=pl.ANY)],
        out_specs=pl.BlockSpec(memory_space=pl.ANY),
        scratch_shapes=[
            pltpu.SemaphoreType.DMA,
            pltpu.SemaphoreType.DMA((n, 2)),
            pltpu.SemaphoreType.DMA((n,)),
        ],
        compiler_params=pltpu.CompilerParams(collective_id=0, has_side_effects=True),
    )(tokens)

    groups = 2
    per_group = rows // groups
    expert = col * experts + jnp.arange(experts, dtype=jnp.int32)
    base = (jnp.arange(total, dtype=jnp.int32) % (total // groups)) * MOST
    slot = seen[:, :, top:] + base[:, None, None] + 1
    match = seen[None, :, :, :top] == expert[:, None, None, None]
    place = jnp.sum(jnp.where(match, slot[None], 0), axis=3) - 1
    place = place.reshape(experts, groups, total // groups * tok).transpose(1, 0, 2)

    order = jnp.arange(total * slots, dtype=jnp.int32)
    dest = order // slots
    held = dest // (total // groups) * experts + order % slots // MOST
    perm = (held * per_group + dest % (total // groups) * MOST + order % MOST)[:, None]
    spot = (chosen * MOST).reshape(tok, top) + rank
    exact = jnp.sum(
        jnp.where(
            spot[:, :, None] == jnp.arange(cols * slots, dtype=jnp.int32), route_weight[:, :, None], 0.0
        ),
        axis=1,
    )
    high = lax.reduce_precision(exact, 8, 7)
    weight = jnp.concatenate([high, exact - high], axis=0).astype(jnp.bfloat16)
    weight = weight.reshape(2 * tok, cols, slots).transpose(1, 0, 2)

    vmem = pl.BlockSpec(memory_space=pltpu.VMEM)
    anywhere = pl.BlockSpec(memory_space=pl.ANY)
    return pl.pallas_call(
        functools.partial(expert_kernel, n, cols, groups),
        out_shape=jax.ShapeDtypeStruct((tok, features), jnp.bfloat16),
        in_specs=[anywhere, vmem, anywhere, anywhere, vmem, vmem],
        out_specs=vmem,
        scratch_shapes=[
            pltpu.VMEM((experts, 2, hidden, features), jnp.bfloat16),
            pltpu.VMEM((experts, n, hidden, width), jnp.bfloat16),
            pltpu.VMEM((total, tok, features), jnp.bfloat16),
            pltpu.VMEM((experts * per_group, total // groups * tok), jnp.bfloat16),
            pltpu.VMEM((experts * per_group, features), jnp.bfloat16),
            pltpu.VMEM((n, groups * experts, per_group, hidden), jnp.bfloat16),
            pltpu.VMEM((experts * rows, width), jnp.bfloat16),
            pltpu.VMEM((total, slots, width), jnp.bfloat16),
            pltpu.VMEM((total, slots, width), jnp.bfloat16),
            pltpu.SemaphoreType.DMA((experts,)),
            pltpu.SemaphoreType.DMA((experts,)),
            pltpu.SemaphoreType.DMA((n,)),
            pltpu.SemaphoreType.DMA((total, 5)),
            pltpu.SemaphoreType.DMA((total, 2)),
            pltpu.SemaphoreType.DMA((n, groups * experts, 2)),
            pltpu.SemaphoreType.DMA((n, groups * experts)),
            pltpu.SemaphoreType.DMA((total,)),
            pltpu.SemaphoreType.DMA((total,)),
        ],
        compiler_params=pltpu.CompilerParams(
            collective_id=1, has_side_effects=True, vmem_limit_bytes=63 * 1024 * 1024
        ),
    )(line, place, expert_in, expert_out.reshape(experts, n, hidden, width), perm, weight)


def solution(mesh):
    n, cols = mesh.shape["dp"], mesh.shape["expert"]

    def body(*args):
        if n * cols > 32 or cols != 8:
            return local(*args)
        return fused(n, cols, *args)

    return jax.shard_map(
        body,
        mesh=mesh,
        in_specs=(
            P(("dp", "expert"), None),
            P(("dp", "expert"), None),
            P(("dp", "expert"), None),
            P("expert", None, "dp", None),
            P("expert", None, "dp"),
        ),
        out_specs=P(("dp", "expert"), None),
        check_vma=False,
    )
```

```python
import functools

import jax
import jax.numpy as jnp
from jax import lax
from jax.experimental import pallas as pl
from jax.experimental.pallas import tpu as pltpu
from jax.sharding import PartitionSpec as P

MOST = 5
LANES = 128
MESH = pl.DeviceIdType.MESH


def slot_parts(route_rows):
    flat = route_rows.reshape(-1)
    order = jnp.arange(flat.shape[0], dtype=jnp.int32)
    earlier = (flat[:, None] == flat[None, :]) & (order[None, :] < order[:, None])
    return (flat, jnp.sum(earlier.astype(jnp.int32), axis=1))


def pack_rows(source_rows, target, owner, slot_count):
    filled = jnp.zeros((slot_count,), jnp.int32).at[target].set(owner + 1)
    picked = source_rows[jnp.maximum(filled - 1, 0)]
    return jnp.where((filled > 0)[:, None], picked, jnp.zeros_like(picked))


def local(tokens, routes, route_weight, expert_in, expert_out):
    dp_count = lax.axis_size("dp")
    col_count = lax.axis_size("expert")
    local_experts = expert_in.shape[0]
    tok_count = tokens.shape[0]
    route_count = routes.shape[1]
    features = tokens.shape[1]
    slice_width = expert_out.shape[2]
    pair_count = tok_count * route_count
    chosen, rank = slot_parts(routes)
    own_slot = chosen % local_experts * (col_count * MOST) + chosen // local_experts * MOST + rank
    owner = jnp.arange(pair_count, dtype=jnp.int32) // route_count
    packed = pack_rows(tokens, own_slot, owner, local_experts * col_count * MOST)
    packed = packed.reshape(local_experts, col_count, MOST * features)
    arrived = lax.all_to_all(packed, "expert", split_axis=1, concat_axis=1, tiled=True)
    arrived = arrived.reshape(local_experts, col_count * MOST, features)
    both = jnp.einsum(
        "erd,egfd->gefr",
        lax.all_gather(arrived, "dp", axis=1, tiled=True),
        expert_in,
        preferred_element_type=jnp.float32,
    )
    hidden = (jax.nn.silu(both[0]) * both[1]).astype(jnp.bfloat16)
    piece = lax.all_gather(hidden, "dp", axis=1, tiled=True)
    width = piece.shape[1]
    blocks = piece.reshape(local_experts, width, dp_count, col_count, MOST)
    outputs = jnp.einsum(
        "efabm,efd->ebmad", blocks, expert_out, preferred_element_type=jnp.float32
    ).astype(jnp.bfloat16)
    outputs = outputs.reshape(local_experts, col_count, MOST, dp_count * slice_width)
    returned = lax.all_to_all(
        lax.all_to_all(outputs, "dp", split_axis=3, concat_axis=3, tiled=True),
        "expert",
        split_axis=1,
        concat_axis=1,
        tiled=True,
    )
    returned = returned.reshape(local_experts * col_count * MOST, features)
    picked = returned[own_slot].reshape(tok_count, route_count, features)
    mixed = jnp.sum(route_weight[:, :, None] * picked.astype(jnp.float32), axis=1)
    return mixed.astype(jnp.bfloat16)


def line_kernel(
    n, cols, own_ref, meta_ref, out_ref, metas_ref,
    own_sem, send_sem, recv_sem, meta_sem, meta_send, meta_recv,
):
    z, c = lax.axis_index("dp"), lax.axis_index("expert")
    me, total = z * cols + c, n * cols
    own = pltpu.make_async_copy(own_ref, out_ref.at[z], own_sem)
    own.start()
    own_meta = pltpu.make_async_copy(meta_ref, metas_ref.at[me], meta_sem)
    own_meta.start()
    barrier = pltpu.get_barrier_semaphore()

    @pl.loop(1, total)
    def _(d):
        other = (me + d) % total
        pl.semaphore_signal(barrier, inc=1, device_id=(other // cols, other % cols), device_id_type=MESH)

    pl.semaphore_wait(barrier, total - 1)

    def tell(other, slot):
        return pltpu.make_async_remote_copy(
            src_ref=meta_ref, dst_ref=metas_ref.at[slot], send_sem=meta_send.at[other],
            recv_sem=meta_recv.at[slot], device_id=(other // cols, other % cols), device_id_type=MESH,
        )

    def copy(zz, way, target, first=False):
        return pltpu.make_async_remote_copy(
            src_ref=own_ref if first else out_ref.at[zz], dst_ref=out_ref.at[zz],
            send_sem=send_sem.at[zz, way], recv_sem=recv_sem.at[zz],
            device_id=(target, c), device_id_type=MESH,
        )

    @pl.when(z < n - 1)
    def _():
        copy(z, 0, z + 1, True).start()

    @pl.when(z > 0)
    def _():
        copy(z, 1, z - 1, True).start()

    @pl.loop(1, total)
    def _(d):
        tell((me + d) % total, me).start()

    for d in range(1, n):
        @pl.when(z - d >= 0)
        def _():
            copy(z - d, 0, (z + 1) % n).wait_recv()

            @pl.when(z < n - 1)
            def _():
                copy(z - d, 0, z + 1).start()

        @pl.when(z + d < n)
        def _():
            copy(z + d, 1, (z + 1) % n).wait_recv()

            @pl.when(z > 0)
            def _():
                copy(z + d, 1, z - 1).start()

    own.wait()
    own_meta.wait()

    @pl.loop(1, total)
    def _(d):
        other = (me + d) % total
        tell(other, other).wait_recv()
        tell(other, me).wait_send()

    for zz in range(n):
        @pl.when((z < n - 1) & (zz <= z))
        def _():
            copy(zz, 0, z + 1).wait_send()

        @pl.when((z > 0) & (zz >= z))
        def _():
            copy(zz, 1, z - 1).wait_send()


def expert_kernel(
    n, cols, groups, line_ref, place_ref, win_ref, wout_ref, perm_ref, weight_ref, out_ref,
    win, wout, tokens, pick, x, hid, outs, msg, got,
    win_sem, wout_sem, own_sem, tok_send, tok_recv, hid_send, hid_recv, msg_send, msg_recv,
):
    z, c = lax.axis_index("dp"), lax.axis_index("expert")
    me = z * cols + c
    total = n * cols
    experts, rows = win.shape[0], hid.shape[2]
    steps = groups * experts
    xn = c + 2 - 4 * ((c // 2) % 2)
    yn = c + 4 - 8 * (c // 4)
    diag = xn + 4 - 8 * (xn // 4)
    sib = c + 1 - 2 * (c % 2)
    half = tokens.shape[1] // 2
    features = win.shape[3]
    width = outs.shape[1]

    barrier = pltpu.get_barrier_semaphore()

    @pl.loop(1, total)
    def _(d):
        other = (me + d) % total
        pl.semaphore_signal(barrier, inc=1, device_id=(other // cols, other % cols), device_id_type=MESH)

    pl.semaphore_wait(barrier, total - 1)

    def own_block(zz):
        return pltpu.make_async_copy(line_ref.at[zz], tokens.at[zz * cols + c], own_sem.at[zz])

    def share(zz, col, kind, target, part=None):
        block = zz * cols + col
        dst, sem = tokens.at[block], tok_recv.at[block, 0]
        src = line_ref.at[zz] if kind < 3 else dst
        if part is not None:
            src = dst = tokens.at[block, pl.ds(part * half, half)]
            sem = tok_recv.at[block, part]
        return pltpu.make_async_remote_copy(
            src_ref=src, dst_ref=dst, send_sem=tok_send.at[block, kind], recv_sem=sem,
            device_id=(z, target), device_id_type=MESH,
        )

    def offer(zz):
        return [share(zz, c, 0, xn), share(zz, c, 1, yn), share(zz, c, 2, sib)]

    def relay(zz):
        return [
            share(zz, xn, 3, yn, 0), share(zz, xn, 4, sib),
            share(zz, yn, 3, xn, 1), share(zz, yn, 4, sib),
        ]

    def begin(zz):
        own_block(zz).start()
        for cp in offer(zz):
            cp.start()

    def forward(zz):
        share(zz, xn, 4, sib).wait_recv()
        for cp in relay(zz)[:2]:
            cp.start()
        share(zz, yn, 4, sib).wait_recv()
        for cp in relay(zz)[2:]:
            cp.start()

    def across(zz):
        share(zz, diag, 3, yn, 0).wait_recv()
        share(zz, diag, 3, xn, 1).wait_recv()
        share(zz, diag, 4, sib).start()

    def complete(zz):
        own_block(zz).wait()
        for col in (sib, xn + 1 - 2 * (xn % 2), yn + 1 - 2 * (yn % 2), diag + 1 - 2 * (diag % 2)):
            share(zz, col, 4, sib).wait_recv()

    per = n // groups
    for zz in range(per):
        begin(zz)
    @pl.loop(0, experts)
    def _(e):
        pltpu.make_async_copy(win_ref.at[e], win.at[e], win_sem.at[e]).start()

    @pl.loop(0, experts)
    def _(e):
        pltpu.make_async_copy(wout_ref.at[e], wout.at[e], wout_sem.at[e]).start()

    for zz in range(per, n):
        begin(zz)
    for zz in range(per):
        forward(zz)
    for zz in range(per):
        across(zz)
    for zz in range(per):
        complete(zz)

    def choose(g):
        size = tokens.shape[1] * per * cols
        for e in range(experts):
            at = lax.broadcasted_iota(jnp.int32, (rows, size), 0)
            named = place_ref[g, e:e + 1, :]
            pick[e * rows:(e + 1) * rows, :] = jnp.where(at == named, 1.0, 0.0).astype(jnp.bfloat16)

        @pl.loop(0, features // width)
        def _(j):
            at = pl.ds(pl.multiple_of(j * width, width), width)
            part = tokens[pl.ds(g * (per * cols), per * cols), :, at].reshape(size, width)
            x[:, at] = jnp.dot(pick[...], part, preferred_element_type=jnp.float32).astype(jnp.bfloat16)

    def pass_on(zz, e, way, target):
        return pltpu.make_async_remote_copy(
            src_ref=hid.at[zz, e], dst_ref=hid.at[zz, e], send_sem=hid_send.at[zz, e, way],
            recv_sem=hid_recv.at[zz, e], device_id=(target, c), device_id_type=MESH,
        )

    def upward(zz, e):
        @pl.when(z < n - 1)
        def _():
            pass_on(zz, e, 0, z + 1).start()

    def downward(zz, e):
        @pl.when(z > 0)
        def _():
            pass_on(zz, e, 1, z - 1).start()

    contract_last = (((1,), (1,)), ((), ()))

    def message(dest):
        return pltpu.make_async_remote_copy(
            src_ref=msg.at[dest], dst_ref=got.at[me], send_sem=msg_send.at[dest],
            recv_sem=msg_recv.at[me], device_id=(dest // cols, dest % cols), device_id_type=MESH,
        )

    slots = msg.shape[1]

    def respond(g):
        @pl.loop(0, per)
        def _(j):
            zz = g * per + j
            part = perm_ref[pl.ds(pl.multiple_of(zz * (cols * slots), cols * slots), cols * slots), :]
            lanes = lax.broadcasted_iota(jnp.int32, (cols * slots, experts * rows), 1)
            take = jnp.where(lanes == part, 1.0, 0.0).astype(jnp.bfloat16)
            held = outs[g * (experts * rows):(g + 1) * (experts * rows), :]
            moved = jnp.dot(take, held, preferred_element_type=jnp.float32)
            msg[pl.ds(zz * cols, cols)] = moved.reshape(cols, slots, width).astype(jnp.bfloat16)

            @pl.loop(0, cols)
            def _(k):
                dest = zz * cols + (c + k) % cols

                @pl.when(dest != me)
                def _():
                    message(dest).start()

    choose(0)

    @pl.loop(0, steps + n - 1)
    def _(i):
        for g in range(1, groups):
            for k in range(per):
                @pl.when(i == (g - 1) * experts + 1 + 2 * k)
                def _():
                    forward(g * per + k)

                @pl.when(i == (g - 1) * experts + 3 + 2 * k)
                def _():
                    across(g * per + k)

            @pl.when(i == g * experts)
            def _():
                for k in range(per):
                    complete(g * per + k)
                choose(g)

        @pl.when(i < experts)
        def _():
            pltpu.make_async_copy(win_ref.at[i], win.at[i], win_sem.at[i]).wait()

        @pl.when(i < steps)
        def _():
            e = i % experts
            xe = x[pl.ds(pl.multiple_of(e * rows, rows), rows), :]
            gate = lax.dot_general(xe, win[e, 0], contract_last, preferred_element_type=jnp.float32)
            up = lax.dot_general(xe, win[e, 1], contract_last, preferred_element_type=jnp.float32)
            hid[z, i] = (gate / (1.0 + jnp.exp(-gate)) * up).astype(jnp.bfloat16)
            upward(z, i)
            downward(z, i)

        for d in range(1, n):
            e = i - d

            @pl.when((e >= 0) & (e < steps) & (z - d >= 0))
            def _():
                pass_on(z - d, e, 0, (z + 1) % n).wait_recv()
                upward(z - d, e)

            @pl.when((e >= 0) & (e < steps) & (z + d < n))
            def _():
                pass_on(z + d, e, 1, (z + 1) % n).wait_recv()
                downward(z + d, e)

        @pl.when(i >= n - 1)
        def _():
            step = i - (n - 1)
            e = step % experts

            @pl.when(step < experts)
            def _():
                pltpu.make_async_copy(wout_ref.at[e], wout.at[e], wout_sem.at[e]).wait()

            acc = jnp.zeros((rows, width), jnp.float32)
            for zz in range(n):
                acc += jnp.dot(hid[zz, step], wout[e, zz], preferred_element_type=jnp.float32)
            row = pl.multiple_of(step * rows, rows)
            outs[pl.ds(row, rows), :] = acc.astype(jnp.bfloat16)

        for g in range(groups - 1):
            @pl.when(i == (g + 1) * experts + n - 2)
            def _():
                respond(g)

    respond(groups - 1)
    got[me] = msg[me]

    @pl.loop(1, total)
    def _(d):
        source = (me + d) % total
        pltpu.make_async_remote_copy(
            src_ref=msg.at[source], dst_ref=got.at[source], send_sem=msg_send.at[source],
            recv_sem=msg_recv.at[source], device_id=(source // cols, source % cols), device_id_type=MESH,
        ).wait_recv()

    tok = out_ref.shape[0]
    for zz in range(n):
        acc = jnp.zeros((2 * tok, width), jnp.float32)
        for col in range(cols):
            acc += jnp.dot(weight_ref[col], got[zz * cols + col], preferred_element_type=jnp.float32)
        out_ref[:, zz * width:(zz + 1) * width] = (acc[:tok] + acc[tok:]).astype(jnp.bfloat16)

    @pl.loop(1, total)
    def _(d):
        message((me + d) % total).wait_send()

    @pl.loop(0, n)
    def _(zz):
        for cp in offer(zz) + relay(zz) + [share(zz, diag, 4, sib)]:
            cp.wait_send()

    @pl.loop(0, steps)
    def _(e):
        for zz in range(n):
            @pl.when((z < n - 1) & (zz <= z))
            def _():
                pass_on(zz, e, 0, z + 1).wait_send()

            @pl.when((z > 0) & (zz >= z))
            def _():
                pass_on(zz, e, 1, z - 1).wait_send()


def fused(n, cols, tokens, routes, route_weight, expert_in, expert_out):
    tok, features = tokens.shape
    top = routes.shape[1]
    experts, _, hidden, _ = expert_in.shape
    width = expert_out.shape[2]
    total = n * cols
    col = lax.axis_index("expert")
    slots = experts * MOST
    rows = total * MOST

    chosen, rank = slot_parts(routes)
    rank = rank.reshape(tok, top)
    meta = jnp.concatenate([routes, rank], axis=1).reshape(-1, LANES)
    filled = meta.shape[0]
    meta = jnp.pad(meta, ((0, -filled % 8), (0, 0)))
    line, metas = pl.pallas_call(
        functools.partial(line_kernel, n, cols),
        out_shape=[
            jax.ShapeDtypeStruct((n, tok, features), jnp.bfloat16),
            jax.ShapeDtypeStruct((total,) + meta.shape, jnp.int32),
        ],
        in_specs=[pl.BlockSpec(memory_space=pl.ANY)] * 2,
        out_specs=[pl.BlockSpec(memory_space=pl.ANY)] * 2,
        scratch_shapes=[
            pltpu.SemaphoreType.DMA,
            pltpu.SemaphoreType.DMA((n, 2)),
            pltpu.SemaphoreType.DMA((n,)),
            pltpu.SemaphoreType.DMA,
            pltpu.SemaphoreType.DMA((total,)),
            pltpu.SemaphoreType.DMA((total,)),
        ],
        compiler_params=pltpu.CompilerParams(collective_id=0, has_side_effects=True),
    )(tokens, meta)
    seen = metas[:, :filled].reshape(total, tok, 2 * top)

    groups = 2
    per_group = rows // groups
    expert = col * experts + jnp.arange(experts, dtype=jnp.int32)
    base = (jnp.arange(total, dtype=jnp.int32) % (total // groups)) * MOST
    slot = seen[:, :, top:] + base[:, None, None] + 1
    match = seen[None, :, :, :top] == expert[:, None, None, None]
    place = jnp.sum(jnp.where(match, slot[None], 0), axis=3) - 1
    place = place.reshape(experts, groups, total // groups * tok).transpose(1, 0, 2)

    order = jnp.arange(total * slots, dtype=jnp.int32)
    dest = order // slots
    held = order % slots // MOST
    perm = (held * per_group + dest % (total // groups) * MOST + order % MOST)[:, None]
    spot = (chosen * MOST).reshape(tok, top) + rank
    exact = jnp.sum(
        jnp.where(
            spot[:, :, None] == jnp.arange(cols * slots, dtype=jnp.int32), route_weight[:, :, None], 0.0
        ),
        axis=1,
    )
    high = lax.reduce_precision(exact, 8, 7)
    weight = jnp.concatenate([high, exact - high], axis=0).astype(jnp.bfloat16)
    weight = weight.reshape(2 * tok, cols, slots).transpose(1, 0, 2)

    vmem = pl.BlockSpec(memory_space=pltpu.VMEM)
    anywhere = pl.BlockSpec(memory_space=pl.ANY)
    return pl.pallas_call(
        functools.partial(expert_kernel, n, cols, groups),
        out_shape=jax.ShapeDtypeStruct((tok, features), jnp.bfloat16),
        in_specs=[anywhere, vmem, anywhere, anywhere, vmem, vmem],
        out_specs=vmem,
        scratch_shapes=[
            pltpu.VMEM((experts, 2, hidden, features), jnp.bfloat16),
            pltpu.VMEM((experts, n, hidden, width), jnp.bfloat16),
            pltpu.VMEM((total, tok, features), jnp.bfloat16),
            pltpu.VMEM((experts * per_group, total // groups * tok), jnp.bfloat16),
            pltpu.VMEM((experts * per_group, features), jnp.bfloat16),
            pltpu.VMEM((n, groups * experts, per_group, hidden), jnp.bfloat16),
            pltpu.VMEM((experts * rows, width), jnp.bfloat16),
            pltpu.VMEM((total, slots, width), jnp.bfloat16),
            pltpu.VMEM((total, slots, width), jnp.bfloat16),
            pltpu.SemaphoreType.DMA((experts,)),
            pltpu.SemaphoreType.DMA((experts,)),
            pltpu.SemaphoreType.DMA((n,)),
            pltpu.SemaphoreType.DMA((total, 5)),
            pltpu.SemaphoreType.DMA((total, 2)),
            pltpu.SemaphoreType.DMA((n, groups * experts, 2)),
            pltpu.SemaphoreType.DMA((n, groups * experts)),
            pltpu.SemaphoreType.DMA((total,)),
            pltpu.SemaphoreType.DMA((total,)),
        ],
        compiler_params=pltpu.CompilerParams(
            collective_id=1, has_side_effects=True, vmem_limit_bytes=63 * 1024 * 1024
        ),
    )(line, place, expert_in, expert_out.reshape(experts, n, hidden, width), perm, weight)


def solution(mesh):
    n, cols = mesh.shape["dp"], mesh.shape["expert"]

    def body(*args):
        if n * cols > 32 or cols != 8:
            return local(*args)
        return fused(n, cols, *args)

    return jax.shard_map(
        body,
        mesh=mesh,
        in_specs=(
            P(("dp", "expert"), None),
            P(("dp", "expert"), None),
            P(("dp", "expert"), None),
            P("expert", None, "dp", None),
            P("expert", None, "dp"),
        ),
        out_specs=P(("dp", "expert"), None),
        check_vma=False,
    )
```

```python
import functools

import jax
import jax.numpy as jnp
from jax import lax
from jax.experimental import pallas as pl
from jax.experimental.pallas import tpu as pltpu
from jax.sharding import PartitionSpec as P

MOST = 5
LANES = 128
MESH = pl.DeviceIdType.MESH


def slot_parts(route_rows):
    flat = route_rows.reshape(-1)
    order = jnp.arange(flat.shape[0], dtype=jnp.int32)
    earlier = (flat[:, None] == flat[None, :]) & (order[None, :] < order[:, None])
    return (flat, jnp.sum(earlier.astype(jnp.int32), axis=1))


def pack_rows(source_rows, target, owner, slot_count):
    filled = jnp.zeros((slot_count,), jnp.int32).at[target].set(owner + 1)
    picked = source_rows[jnp.maximum(filled - 1, 0)]
    return jnp.where((filled > 0)[:, None], picked, jnp.zeros_like(picked))


def local(tokens, routes, route_weight, expert_in, expert_out):
    dp_count = lax.axis_size("dp")
    col_count = lax.axis_size("expert")
    local_experts = expert_in.shape[0]
    tok_count = tokens.shape[0]
    route_count = routes.shape[1]
    features = tokens.shape[1]
    slice_width = expert_out.shape[2]
    pair_count = tok_count * route_count
    chosen, rank = slot_parts(routes)
    own_slot = chosen % local_experts * (col_count * MOST) + chosen // local_experts * MOST + rank
    owner = jnp.arange(pair_count, dtype=jnp.int32) // route_count
    packed = pack_rows(tokens, own_slot, owner, local_experts * col_count * MOST)
    packed = packed.reshape(local_experts, col_count, MOST * features)
    arrived = lax.all_to_all(packed, "expert", split_axis=1, concat_axis=1, tiled=True)
    arrived = arrived.reshape(local_experts, col_count * MOST, features)
    both = jnp.einsum(
        "erd,egfd->gefr",
        lax.all_gather(arrived, "dp", axis=1, tiled=True),
        expert_in,
        preferred_element_type=jnp.float32,
    )
    hidden = (jax.nn.silu(both[0]) * both[1]).astype(jnp.bfloat16)
    piece = lax.all_gather(hidden, "dp", axis=1, tiled=True)
    width = piece.shape[1]
    blocks = piece.reshape(local_experts, width, dp_count, col_count, MOST)
    outputs = jnp.einsum(
        "efabm,efd->ebmad", blocks, expert_out, preferred_element_type=jnp.float32
    ).astype(jnp.bfloat16)
    outputs = outputs.reshape(local_experts, col_count, MOST, dp_count * slice_width)
    returned = lax.all_to_all(
        lax.all_to_all(outputs, "dp", split_axis=3, concat_axis=3, tiled=True),
        "expert",
        split_axis=1,
        concat_axis=1,
        tiled=True,
    )
    returned = returned.reshape(local_experts * col_count * MOST, features)
    picked = returned[own_slot].reshape(tok_count, route_count, features)
    mixed = jnp.sum(route_weight[:, :, None] * picked.astype(jnp.float32), axis=1)
    return mixed.astype(jnp.bfloat16)


def line_kernel(
    n, cols, own_ref, meta_ref, out_ref, metas_ref,
    own_sem, send_sem, recv_sem, meta_sem, meta_send, meta_recv,
):
    z, c = lax.axis_index("dp"), lax.axis_index("expert")
    me, total = z * cols + c, n * cols
    own = pltpu.make_async_copy(own_ref, out_ref.at[z], own_sem)
    own.start()
    own_meta = pltpu.make_async_copy(meta_ref, metas_ref.at[me], meta_sem)
    own_meta.start()
    barrier = pltpu.get_barrier_semaphore()

    @pl.loop(1, total)
    def _(d):
        other = (me + d) % total
        pl.semaphore_signal(barrier, inc=1, device_id=(other // cols, other % cols), device_id_type=MESH)

    pl.semaphore_wait(barrier, total - 1)

    def tell(other, slot):
        return pltpu.make_async_remote_copy(
            src_ref=meta_ref, dst_ref=metas_ref.at[slot], send_sem=meta_send.at[other],
            recv_sem=meta_recv.at[slot], device_id=(other // cols, other % cols), device_id_type=MESH,
        )

    def copy(zz, way, target, first=False):
        return pltpu.make_async_remote_copy(
            src_ref=own_ref if first else out_ref.at[zz], dst_ref=out_ref.at[zz],
            send_sem=send_sem.at[zz, way], recv_sem=recv_sem.at[zz],
            device_id=(target, c), device_id_type=MESH,
        )

    @pl.when(z < n - 1)
    def _():
        copy(z, 0, z + 1, True).start()

    @pl.when(z > 0)
    def _():
        copy(z, 1, z - 1, True).start()

    @pl.loop(1, total)
    def _(d):
        tell((me + d) % total, me).start()

    for d in range(1, n):
        @pl.when(z - d >= 0)
        def _():
            copy(z - d, 0, (z + 1) % n).wait_recv()

            @pl.when(z < n - 1)
            def _():
                copy(z - d, 0, z + 1).start()

        @pl.when(z + d < n)
        def _():
            copy(z + d, 1, (z + 1) % n).wait_recv()

            @pl.when(z > 0)
            def _():
                copy(z + d, 1, z - 1).start()

    own.wait()
    own_meta.wait()

    @pl.loop(1, total)
    def _(d):
        other = (me + d) % total
        tell(other, other).wait_recv()
        tell(other, me).wait_send()

    for zz in range(n):
        @pl.when((z < n - 1) & (zz <= z))
        def _():
            copy(zz, 0, z + 1).wait_send()

        @pl.when((z > 0) & (zz >= z))
        def _():
            copy(zz, 1, z - 1).wait_send()


def expert_kernel(
    n, cols, groups, line_ref, place_ref, win_ref, wout_ref, perm_ref, weight_ref, out_ref,
    win, wout, tokens, pick, x, hid, outs, msg, got,
    win_sem, wout_sem, own_sem, tok_send, tok_recv, hid_send, hid_recv, msg_send, msg_recv,
):
    z, c = lax.axis_index("dp"), lax.axis_index("expert")
    me = z * cols + c
    total = n * cols
    experts, rows = win.shape[0], hid.shape[2]
    steps = groups * experts
    xn = c + 2 - 4 * ((c // 2) % 2)
    yn = c + 4 - 8 * (c // 4)
    diag = xn + 4 - 8 * (xn // 4)
    sib = c + 1 - 2 * (c % 2)
    half = tokens.shape[1] // 2
    features = win.shape[3]
    width = outs.shape[1]

    barrier = pltpu.get_barrier_semaphore()

    @pl.loop(1, total)
    def _(d):
        other = (me + d) % total
        pl.semaphore_signal(barrier, inc=1, device_id=(other // cols, other % cols), device_id_type=MESH)

    pl.semaphore_wait(barrier, total - 1)

    def own_block(zz):
        return pltpu.make_async_copy(line_ref.at[zz], tokens.at[zz * cols + c], own_sem.at[zz])

    def share(zz, col, kind, target, part=None):
        block = zz * cols + col
        dst, sem = tokens.at[block], tok_recv.at[block, 0]
        src = line_ref.at[zz] if kind < 3 else dst
        if part is not None:
            src = dst = tokens.at[block, pl.ds(part * half, half)]
            sem = tok_recv.at[block, part]
        return pltpu.make_async_remote_copy(
            src_ref=src, dst_ref=dst, send_sem=tok_send.at[block, kind], recv_sem=sem,
            device_id=(z, target), device_id_type=MESH,
        )

    def offer(zz):
        return [share(zz, c, 0, xn), share(zz, c, 1, yn), share(zz, c, 2, sib)]

    def relay(zz):
        return [
            share(zz, xn, 3, yn, 0), share(zz, xn, 4, sib),
            share(zz, yn, 3, xn, 1), share(zz, yn, 4, sib),
        ]

    def begin(zz):
        own_block(zz).start()
        for cp in offer(zz):
            cp.start()

    def forward(zz):
        share(zz, xn, 4, sib).wait_recv()
        for cp in relay(zz)[:2]:
            cp.start()
        share(zz, yn, 4, sib).wait_recv()
        for cp in relay(zz)[2:]:
            cp.start()

    def across(zz):
        share(zz, diag, 3, yn, 0).wait_recv()
        share(zz, diag, 3, xn, 1).wait_recv()
        share(zz, diag, 4, sib).start()

    def complete(zz):
        own_block(zz).wait()
        for col in (sib, xn + 1 - 2 * (xn % 2), yn + 1 - 2 * (yn % 2), diag + 1 - 2 * (diag % 2)):
            share(zz, col, 4, sib).wait_recv()

    per = n // groups
    for zz in range(per):
        begin(zz)
    @pl.loop(0, experts)
    def _(e):
        pltpu.make_async_copy(win_ref.at[e], win.at[e], win_sem.at[e]).start()

    @pl.loop(0, experts)
    def _(e):
        pltpu.make_async_copy(wout_ref.at[e], wout.at[e], wout_sem.at[e]).start()

    for zz in range(per, n):
        begin(zz)
    for zz in range(per):
        forward(zz)
    for zz in range(per):
        across(zz)
    for zz in range(per):
        complete(zz)

    def choose(g):
        size = tokens.shape[1] * per * cols
        for e in range(experts):
            at = lax.broadcasted_iota(jnp.int32, (rows, size), 0)
            named = place_ref[g, e:e + 1, :]
            pick[e * rows:(e + 1) * rows, :] = jnp.where(at == named, 1.0, 0.0).astype(jnp.bfloat16)

        @pl.loop(0, features // width)
        def _(j):
            at = pl.ds(pl.multiple_of(j * width, width), width)
            part = tokens[pl.ds(g * (per * cols), per * cols), :, at].reshape(size, width)
            x[:, at] = jnp.dot(pick[...], part, preferred_element_type=jnp.float32).astype(jnp.bfloat16)

    def pass_on(zz, e, way, target):
        return pltpu.make_async_remote_copy(
            src_ref=hid.at[zz, e], dst_ref=hid.at[zz, e], send_sem=hid_send.at[zz, e, way],
            recv_sem=hid_recv.at[zz, e], device_id=(target, c), device_id_type=MESH,
        )

    def upward(zz, e):
        @pl.when(z < n - 1)
        def _():
            pass_on(zz, e, 0, z + 1).start()

    def downward(zz, e):
        @pl.when(z > 0)
        def _():
            pass_on(zz, e, 1, z - 1).start()

    contract_last = (((1,), (1,)), ((), ()))

    def message(dest):
        return pltpu.make_async_remote_copy(
            src_ref=msg.at[dest], dst_ref=got.at[me], send_sem=msg_send.at[dest],
            recv_sem=msg_recv.at[me], device_id=(dest // cols, dest % cols), device_id_type=MESH,
        )

    slots = msg.shape[1]

    def respond(g):
        @pl.loop(0, per)
        def _(j):
            zz = g * per + j
            part = perm_ref[pl.ds(pl.multiple_of(zz * (cols * slots), cols * slots), cols * slots), :]
            lanes = lax.broadcasted_iota(jnp.int32, (cols * slots, experts * rows), 1)
            take = jnp.where(lanes == part, 1.0, 0.0).astype(jnp.bfloat16)
            held = outs[g * (experts * rows):(g + 1) * (experts * rows), :]
            moved = jnp.dot(take, held, preferred_element_type=jnp.float32)
            msg[pl.ds(zz * cols, cols)] = moved.reshape(cols, slots, width).astype(jnp.bfloat16)

            @pl.loop(0, cols)
            def _(k):
                dest = zz * cols + (c + k) % cols

                @pl.when(dest != me)
                def _():
                    message(dest).start()

    choose(0)

    @pl.loop(0, steps + n - 1)
    def _(i):
        for g in range(1, groups):
            for k in range(per):
                @pl.when(i == (g - 1) * experts + 1 + 2 * k)
                def _():
                    forward(g * per + k)

                @pl.when(i == (g - 1) * experts + 3 + 2 * k)
                def _():
                    across(g * per + k)

            @pl.when(i == g * experts)
            def _():
                for k in range(per):
                    complete(g * per + k)
                choose(g)

        @pl.when(i < experts)
        def _():
            pltpu.make_async_copy(win_ref.at[i], win.at[i], win_sem.at[i]).wait()

        @pl.when(i < steps)
        def _():
            e = i % experts
            xe = x[pl.ds(pl.multiple_of(e * rows, rows), rows), :]
            gate = lax.dot_general(xe, win[e, 0], contract_last, preferred_element_type=jnp.float32)
            up = lax.dot_general(xe, win[e, 1], contract_last, preferred_element_type=jnp.float32)
            hid[z, i] = (gate / (1.0 + jnp.exp(-gate)) * up).astype(jnp.bfloat16)
            upward(z, i)
            downward(z, i)

        for d in range(1, n):
            e = i - d

            @pl.when((e >= 0) & (e < steps) & (z - d >= 0))
            def _():
                pass_on(z - d, e, 0, (z + 1) % n).wait_recv()
                upward(z - d, e)

            @pl.when((e >= 0) & (e < steps) & (z + d < n))
            def _():
                pass_on(z + d, e, 1, (z + 1) % n).wait_recv()
                downward(z + d, e)

        @pl.when(i >= n - 1)
        def _():
            step = i - (n - 1)
            e = step % experts

            @pl.when(step < experts)
            def _():
                pltpu.make_async_copy(wout_ref.at[e], wout.at[e], wout_sem.at[e]).wait()

            acc = jnp.zeros((rows, width), jnp.float32)
            for zz in range(n):
                acc += jnp.dot(hid[zz, step], wout[e, zz], preferred_element_type=jnp.float32)
            row = pl.multiple_of(step * rows, rows)
            outs[pl.ds(row, rows), :] = acc.astype(jnp.bfloat16)

    for g in range(groups):
        respond(g)
    got[me] = msg[me]

    @pl.loop(1, total)
    def _(d):
        source = (me + d) % total
        pltpu.make_async_remote_copy(
            src_ref=msg.at[source], dst_ref=got.at[source], send_sem=msg_send.at[source],
            recv_sem=msg_recv.at[source], device_id=(source // cols, source % cols), device_id_type=MESH,
        ).wait_recv()

    tok = out_ref.shape[0]
    for zz in range(n):
        acc = jnp.zeros((2 * tok, width), jnp.float32)
        for col in range(cols):
            acc += jnp.dot(weight_ref[col], got[zz * cols + col], preferred_element_type=jnp.float32)
        out_ref[:, zz * width:(zz + 1) * width] = (acc[:tok] + acc[tok:]).astype(jnp.bfloat16)

    @pl.loop(1, total)
    def _(d):
        message((me + d) % total).wait_send()

    @pl.loop(0, n)
    def _(zz):
        for cp in offer(zz) + relay(zz) + [share(zz, diag, 4, sib)]:
            cp.wait_send()

    @pl.loop(0, steps)
    def _(e):
        for zz in range(n):
            @pl.when((z < n - 1) & (zz <= z))
            def _():
                pass_on(zz, e, 0, z + 1).wait_send()

            @pl.when((z > 0) & (zz >= z))
            def _():
                pass_on(zz, e, 1, z - 1).wait_send()


def fused(n, cols, tokens, routes, route_weight, expert_in, expert_out):
    tok, features = tokens.shape
    top = routes.shape[1]
    experts, _, hidden, _ = expert_in.shape
    width = expert_out.shape[2]
    total = n * cols
    col = lax.axis_index("expert")
    slots = experts * MOST
    rows = total * MOST

    chosen, rank = slot_parts(routes)
    rank = rank.reshape(tok, top)
    meta = jnp.concatenate([routes, rank], axis=1).reshape(-1, LANES)
    filled = meta.shape[0]
    meta = jnp.pad(meta, ((0, -filled % 8), (0, 0)))
    line, metas = pl.pallas_call(
        functools.partial(line_kernel, n, cols),
        out_shape=[
            jax.ShapeDtypeStruct((n, tok, features), jnp.bfloat16),
            jax.ShapeDtypeStruct((total,) + meta.shape, jnp.int32),
        ],
        in_specs=[pl.BlockSpec(memory_space=pl.ANY)] * 2,
        out_specs=[pl.BlockSpec(memory_space=pl.ANY)] * 2,
        scratch_shapes=[
            pltpu.SemaphoreType.DMA,
            pltpu.SemaphoreType.DMA((n, 2)),
            pltpu.SemaphoreType.DMA((n,)),
            pltpu.SemaphoreType.DMA,
            pltpu.SemaphoreType.DMA((total,)),
            pltpu.SemaphoreType.DMA((total,)),
        ],
        compiler_params=pltpu.CompilerParams(collective_id=0, has_side_effects=True),
    )(tokens, meta)
    seen = metas[:, :filled].reshape(total, tok, 2 * top)

    groups = 2
    per_group = rows // groups
    expert = col * experts + jnp.arange(experts, dtype=jnp.int32)
    base = (jnp.arange(total, dtype=jnp.int32) % (total // groups)) * MOST
    slot = seen[:, :, top:] + base[:, None, None] + 1
    match = seen[None, :, :, :top] == expert[:, None, None, None]
    place = jnp.sum(jnp.where(match, slot[None], 0), axis=3) - 1
    place = place.reshape(experts, groups, total // groups * tok).transpose(1, 0, 2)

    order = jnp.arange(total * slots, dtype=jnp.int32)
    dest = order // slots
    held = order % slots // MOST
    perm = (held * per_group + dest % (total // groups) * MOST + order % MOST)[:, None]
    spot = (chosen * MOST).reshape(tok, top) + rank
    exact = jnp.sum(
        jnp.where(
            spot[:, :, None] == jnp.arange(cols * slots, dtype=jnp.int32), route_weight[:, :, None], 0.0
        ),
        axis=1,
    )
    high = lax.reduce_precision(exact, 8, 7)
    weight = jnp.concatenate([high, exact - high], axis=0).astype(jnp.bfloat16)
    weight = weight.reshape(2 * tok, cols, slots).transpose(1, 0, 2)

    vmem = pl.BlockSpec(memory_space=pltpu.VMEM)
    anywhere = pl.BlockSpec(memory_space=pl.ANY)
    return pl.pallas_call(
        functools.partial(expert_kernel, n, cols, groups),
        out_shape=jax.ShapeDtypeStruct((tok, features), jnp.bfloat16),
        in_specs=[anywhere, vmem, anywhere, anywhere, vmem, vmem],
        out_specs=vmem,
        scratch_shapes=[
            pltpu.VMEM((experts, 2, hidden, features), jnp.bfloat16),
            pltpu.VMEM((experts, n, hidden, width), jnp.bfloat16),
            pltpu.VMEM((total, tok, features), jnp.bfloat16),
            pltpu.VMEM((experts * per_group, total // groups * tok), jnp.bfloat16),
            pltpu.VMEM((experts * per_group, features), jnp.bfloat16),
            pltpu.VMEM((n, groups * experts, per_group, hidden), jnp.bfloat16),
            pltpu.VMEM((experts * rows, width), jnp.bfloat16),
            pltpu.VMEM((total, slots, width), jnp.bfloat16),
            pltpu.VMEM((total, slots, width), jnp.bfloat16),
            pltpu.SemaphoreType.DMA((experts,)),
            pltpu.SemaphoreType.DMA((experts,)),
            pltpu.SemaphoreType.DMA((n,)),
            pltpu.SemaphoreType.DMA((total, 5)),
            pltpu.SemaphoreType.DMA((total, 2)),
            pltpu.SemaphoreType.DMA((n, groups * experts, 2)),
            pltpu.SemaphoreType.DMA((n, groups * experts)),
            pltpu.SemaphoreType.DMA((total,)),
            pltpu.SemaphoreType.DMA((total,)),
        ],
        compiler_params=pltpu.CompilerParams(
            collective_id=1, has_side_effects=True, vmem_limit_bytes=63 * 1024 * 1024
        ),
    )(line, place, expert_in, expert_out.reshape(experts, n, hidden, width), perm, weight)


def solution(mesh):
    n, cols = mesh.shape["dp"], mesh.shape["expert"]

    def body(*args):
        if n * cols > 32 or cols != 8:
            return local(*args)
        return fused(n, cols, *args)

    return jax.shard_map(
        body,
        mesh=mesh,
        in_specs=(
            P(("dp", "expert"), None),
            P(("dp", "expert"), None),
            P(("dp", "expert"), None),
            P("expert", None, "dp", None),
            P("expert", None, "dp"),
        ),
        out_specs=P(("dp", "expert"), None),
        check_vma=False,
    )
```
